512 devices in a mesh: grp: 16 (over y_lo, z), blk: 32 (over x, y_hi, core).
Axes of the slice: x: 4, y: 8 (y_hi: 4, y_lo: 2; y = y_hi * 2 + y_lo), z: 8, core: 2. Of those that a mesh axis runs over, the one named last changes fastest.
Arguments:
- image_embed: bfloat16 [262144, 1152], P(('grp', 'blk')), may hold values from -2 to 2
- text_embed: bfloat16 [262144, 1152], P(('grp', 'blk')), may hold values from -2 to 2
- log_scale: float32 [1], replicated, may hold values from 1.5 to 2.5
- bias: float32 [1], replicated, may hold values from -4 to -2
Outputs:
- image_grad: bfloat16 [262144, 1152], P(('grp', 'blk'))
- text_grad: bfloat16 [262144, 1152], P(('grp', 'blk'))
- row_loss: float32 [262144], P(('grp', 'blk'))
The draws below stay inside these ranges and needn't reach their ends.
All inputs are finite; a program needn't handle non-finite values.
Results may differ from the reference program's by a relative error of at most 0.0063.
Values may be sent and summed in bfloat16 or wider, within the bound.
No kernel may reach another device: no remote copies, remote signals or barrier semaphores. Data moves between devices by JAX's collectives and lax.ppermute only.
A program may use at most 64 MiB of HBM per device.

```python
import math
import jax
import jax.numpy as jnp
from jax import lax

D = 1152
ROWS_DEV = 512
ROWS = 262144
N_GRP = 16
N_BLK = 32


def draw_image_embed(key, part):
    key = jax.random.fold_in(key, 11)
    entry_key, scale_key = jax.random.split(key)
    entries = jnp.clip(jax.random.normal(entry_key, (ROWS, D), jnp.float32), -3.0, 3.0)
    lowest = 0.5
    highest = 5.0
    row_scale = jnp.exp(jax.random.uniform(scale_key, (ROWS, 1), jnp.float32, math.log(lowest), math.log(highest)))
    return (entries * row_scale / math.sqrt(D)).astype(jnp.bfloat16)


def draw_text_embed(key, part):
    key = jax.random.fold_in(key, 23)
    entry_key, scale_key = jax.random.split(key)
    entries = jnp.clip(jax.random.normal(entry_key, (ROWS, D), jnp.float32), -3.0, 3.0)
    lowest = 0.5
    highest = 5.0
    row_scale = jnp.exp(jax.random.uniform(scale_key, (ROWS, 1), jnp.float32, math.log(lowest), math.log(highest)))
    return (entries * row_scale / math.sqrt(D)).astype(jnp.bfloat16)


def setup_inputs(seed: int = 0) -> dict:
    arg_keys = jax.random.split(jax.random.key(seed), 5)
    return {
        "image_embed": draw_image_embed(jax.random.fold_in(arg_keys[4], 71), 0),
        "text_embed": draw_text_embed(jax.random.fold_in(arg_keys[4], 71), 0),
        "log_scale": jnp.clip(jax.random.uniform(arg_keys[2], (1,), jnp.float32, 1.5, 2.5), 1.5, 2.5),
        "bias": jnp.clip(jax.random.uniform(arg_keys[3], (1,), jnp.float32, -4.0, -2.0), -4.0, -2.0),
    }


def unit_rows(values):
    widened = values.astype(jnp.float32)
    inverse = lax.rsqrt(lax.optimization_barrier(jnp.sum(widened * widened, axis=1, keepdims=True)) + 1e-06)
    return (widened * inverse, inverse)

def logit_weights(scores, logit_scale, logit_bias, positive):
    logits = logit_scale * scores + logit_bias
    weights = (logit_scale * (jax.nn.sigmoid(logits) - positive)).astype(jnp.bfloat16)
    return (weights, logits)

def tangent(units, inverse, summed):
    inner = lax.optimization_barrier(jnp.sum(units * summed, axis=1, keepdims=True))
    return (inverse * (summed - units * inner)).astype(jnp.bfloat16)

def rows_dot(left_rows, right_rows):
    return lax.dot_general(left_rows, right_rows, (((1,), (1,)), ((), ())), preferred_element_type=jnp.float32)

def cols_dot(left_rows, right_rows):
    return lax.dot_general(left_rows, right_rows, (((0,), (0,)), ((), ())), preferred_element_type=jnp.float32)

def reference(image_embed, text_embed, log_scale, bias):
    image_units, image_inverse = unit_rows(image_embed)
    text_units, text_inverse = unit_rows(text_embed)
    image_low = image_units.astype(jnp.bfloat16).reshape(N_GRP, N_BLK, ROWS_DEV, D)
    text_low = text_units.astype(jnp.bfloat16).reshape(N_GRP, N_BLK, ROWS_DEV, D)
    image_unit_blocks = image_units.reshape(N_GRP, N_BLK, ROWS_DEV, D)
    text_unit_blocks = text_units.reshape(N_GRP, N_BLK, ROWS_DEV, D)
    image_inv_blocks = image_inverse.reshape(N_GRP, N_BLK, ROWS_DEV, 1)
    text_inv_blocks = text_inverse.reshape(N_GRP, N_BLK, ROWS_DEV, 1)
    logit_scale = jnp.exp(log_scale[0])
    logit_bias = bias[0]
    diagonal = (jnp.arange(ROWS_DEV, dtype=jnp.int32)[:, None] == jnp.arange(4 * ROWS_DEV, dtype=jnp.int32)[None, :]).astype(jnp.float32)
    own_diagonal = diagonal[:, :ROWS_DEV]

    def image_side(index):
        group = index // N_BLK
        column = index % N_BLK
        visiting = jnp.concatenate([text_low[group, column], text_low[group, (column - 1) % N_BLK], text_low[group, (column + 1) % N_BLK], text_low[(group - 1) % N_GRP, column]], axis=0)
        scores = rows_dot(image_low[group, column], visiting)
        weights, logits = logit_weights(scores, logit_scale, logit_bias, diagonal)
        losses = lax.optimization_barrier(jnp.mean(jax.nn.softplus(jnp.where(diagonal > 0, -logits, logits)), axis=1))
        image_sum = jnp.dot(weights, visiting, preferred_element_type=jnp.float32)
        return (tangent(image_unit_blocks[group, column], image_inv_blocks[group, column], image_sum), losses)

    def text_side(index):
        group = index // N_BLK
        column = index % N_BLK
        text_block = text_low[group, column]
        own_image = image_low[group, column]
        own_weights, _ = logit_weights(rows_dot(own_image, text_block), logit_scale, logit_bias, own_diagonal)
        text_sum = cols_dot(own_weights, own_image)
        for image_block in (image_low[group, (column + 1) % N_BLK], image_low[group, (column - 1) % N_BLK], image_low[(group + 1) % N_GRP, column]):
            other_weights, _ = logit_weights(rows_dot(image_block, text_block), logit_scale, logit_bias, 0.0)
            other_part = cols_dot(other_weights, image_block).astype(jnp.bfloat16)
            text_sum = text_sum + other_part.astype(jnp.float32)
        return tangent(text_unit_blocks[group, column], text_inv_blocks[group, column], text_sum)
    indices = jnp.arange(N_GRP * N_BLK, dtype=jnp.int32)
    image_grad, row_loss = lax.map(image_side, indices)
    text_grad = lax.map(text_side, indices)
    return (image_grad.reshape(ROWS, D), text_grad.reshape(ROWS, D), row_loss.reshape(ROWS))
```

```python
import jax
import jax.numpy as jnp
from jax import lax
from jax.experimental import pallas as pl
from jax.experimental.pallas import tpu as pltpu
from jax.sharding import PartitionSpec as P

AXES = ("grp", "blk")
N_GRP = 16
N_BLK = 32
PLANES = 8
TILE = 256
VMEM = pl.BlockSpec(memory_space=pltpu.VMEM)
SMEM = pl.BlockSpec(memory_space=pltpu.SMEM)


def pairs(target):
    found = []
    for group in range(N_GRP):
        for block in range(N_BLK):
            to = target(group, block)
            if to is not None:
                found.append((group * N_BLK + block, (to[0] % N_GRP) * N_BLK + to[1] % N_BLK))
    return found


def send(array, target):
    return lax.ppermute(array, AXES, pairs(target))


def chip_mate(group, block):
    return (group, block ^ 1)


def across(group, block):
    return (group, block + 1 if block % 2 else block - 1)


def unit_rows(values):
    widened = values.astype(jnp.float32)
    inverse = lax.rsqrt(jnp.sum(widened * widened, axis=1, keepdims=True) + 1e-06)
    return (widened * inverse, inverse)


def normalize_into(low_ref, raw):
    low_ref[...] = unit_rows(raw)[0].astype(jnp.bfloat16)


def scale_of(scale_ref):
    return jnp.exp(jnp.full((1, 1), scale_ref[0], jnp.float32))


def weights_of(logits, scale):
    return scale * jax.nn.sigmoid(logits)


def logits_of(left, right, scale, bias):
    scores = lax.dot_general(left, right, (((1,), (1,)), ((), ())), preferred_element_type=jnp.float32)
    return scale * scores + bias


def softplus(logits):
    return jnp.maximum(logits, 0.0) + jnp.log1p(jnp.exp(-jnp.abs(logits)))


def lane_groups(values):
    total = values[:, :128]
    for start in range(128, values.shape[1], 128):
        total = total + values[:, start : start + 128]
    return total


def tangent(raw, summed):
    units, inverse = unit_rows(raw)
    inner = jnp.sum(units * summed, axis=1, keepdims=True)
    return (inverse * (summed - units * inner)).astype(jnp.bfloat16)


def diagonal(start, shape):
    rows = lax.broadcasted_iota(jnp.int32, shape, 0) + start
    return rows == lax.broadcasted_iota(jnp.int32, shape, 1)


def dot(left, right):
    return jnp.dot(left, right, preferred_element_type=jnp.float32)


def own_kernel(
    scale_ref, bias_ref, image_ref, text_ref, image_in_ref, text_in_ref,
    image_low_ref, text_low_ref, image_sum_ref, text_sum_ref, loss_ref, image_in_low, text_in_low,
):
    scale = scale_of(scale_ref)
    bias = bias_ref[0]
    normalize_into(image_low_ref, image_ref[...])
    normalize_into(text_low_ref, text_ref[...])
    normalize_into(image_in_low, image_in_ref[...])
    normalize_into(text_in_low, text_in_ref[...])

    @pl.loop(0, image_ref.shape[0] // TILE)
    def _(step):
        start = pl.multiple_of(step * TILE, TILE)
        here = pl.ds(start, TILE)
        image_low = image_low_ref[here, :]
        text_low = text_low_ref[here, :]
        logits = logits_of(image_low, text_low_ref[...], scale, bias)
        paired = diagonal(start, logits.shape)
        loss = lane_groups(softplus(jnp.where(paired, -logits, logits)))
        weights = (weights_of(logits, scale) - jnp.where(paired, scale, 0.0)).astype(jnp.bfloat16)
        image_sum = dot(weights, text_low_ref[...])
        logits = logits_of(image_low, text_in_low[...], scale, bias)
        loss_ref[here, :] = loss + lane_groups(softplus(logits))
        weights = weights_of(logits, scale).astype(jnp.bfloat16)
        image_sum_ref[here, :] = image_sum + dot(weights, text_in_low[...])
        logits = logits_of(text_low, image_low_ref[...], scale, bias)
        paired = diagonal(start, logits.shape)
        weights = (weights_of(logits, scale) - jnp.where(paired, scale, 0.0)).astype(jnp.bfloat16)
        text_sum = dot(weights, image_low_ref[...])
        logits = logits_of(text_low, image_in_low[...], scale, bias)
        weights = weights_of(logits, scale).astype(jnp.bfloat16)
        text_sum_ref[here, :] = text_sum + dot(weights, image_in_low[...])


def text_kernel(
    scale_ref, bias_ref, text_y_ref, image_low_ref, image_sum_in, loss_in, image_sum_ref, loss_ref, low,
):
    scale = scale_of(scale_ref)
    bias = bias_ref[0]
    normalize_into(low, text_y_ref[...])

    @pl.loop(0, image_low_ref.shape[0] // TILE)
    def _(step):
        here = pl.ds(pl.multiple_of(step * TILE, TILE), TILE)
        logits = logits_of(image_low_ref[here, :], low[...], scale, bias)
        loss_ref[here, :] = loss_in[here, :] + lane_groups(softplus(logits))
        weights = weights_of(logits, scale).astype(jnp.bfloat16)
        image_sum_ref[here, :] = image_sum_in[here, :] + dot(weights, low[...])


def group_kernel(
    scale_ref, bias_ref, text_z_ref, image_z_ref, image_ref, image_low_ref, text_low_ref, image_sum_ref, text_sum_in,
    loss_in, image_grad_ref, text_sum_ref, loss_ref, image_z_low, text_z_low,
):
    scale = scale_of(scale_ref)
    bias = bias_ref[0]
    normalize_into(text_z_low, text_z_ref[...])
    normalize_into(image_z_low, image_z_ref[...])
    columns = 4 * image_ref.shape[0]

    @pl.loop(0, image_ref.shape[0] // TILE)
    def _(step):
        here = pl.ds(pl.multiple_of(step * TILE, TILE), TILE)
        logits = logits_of(image_low_ref[here, :], text_z_low[...], scale, bias)
        loss = loss_in[here, :] + lane_groups(softplus(logits))
        loss_ref[here, :] = jnp.sum(loss, axis=1, keepdims=True) * (1.0 / columns)
        weights = weights_of(logits, scale).astype(jnp.bfloat16)
        image_sum = image_sum_ref[here, :] + dot(weights, text_z_low[...])
        image_grad_ref[here, :] = tangent(image_ref[here, :], image_sum)
        logits = logits_of(text_low_ref[here, :], image_z_low[...], scale, bias)
        weights = weights_of(logits, scale).astype(jnp.bfloat16)
        text_sum_ref[here, :] = text_sum_in[here, :] + dot(weights, image_z_low[...])


def last_kernel(scale_ref, bias_ref, image_y_ref, text_ref, text_low_ref, text_sum_ref, text_grad_ref, low):
    scale = scale_of(scale_ref)
    bias = bias_ref[0]
    normalize_into(low, image_y_ref[...])

    @pl.loop(0, text_ref.shape[0] // TILE)
    def _(step):
        here = pl.ds(pl.multiple_of(step * TILE, TILE), TILE)
        logits = logits_of(text_low_ref[here, :], low[...], scale, bias)
        weights = weights_of(logits, scale).astype(jnp.bfloat16)
        text_sum = text_sum_ref[here, :] + dot(weights, low[...])
        text_grad_ref[here, :] = tangent(text_ref[here, :], text_sum)


def call(kernel, outs, scratch, scalars, arrays):
    return pl.pallas_call(
        kernel,
        out_shape=outs,
        in_specs=[SMEM] * len(scalars) + [VMEM] * len(arrays),
        out_specs=tuple(VMEM for _ in outs),
        scratch_shapes=scratch,
        compiler_params=pltpu.CompilerParams(vmem_limit_bytes=40 * 1024 * 1024),
        cost_estimate=pl.CostEstimate(flops=1000, bytes_accessed=1000, transcendentals=0),
    )(*scalars, *arrays)


def on_device(image_embed, text_embed, log_scale, bias):
    rows, width = image_embed.shape
    low = jax.ShapeDtypeStruct((rows, width), jnp.bfloat16)
    wide = jax.ShapeDtypeStruct((rows, width), jnp.float32)
    lanes = jax.ShapeDtypeStruct((rows, 128), jnp.float32)
    held = pltpu.VMEM((rows, width), jnp.bfloat16)
    scalars = (log_scale, bias)

    text_y = send(text_embed, across)
    image_y = send(image_embed, across)
    text_z = send(text_embed, lambda group, block: (group + 1, block))
    image_z = send(image_embed, lambda group, block: (group - 1, block))
    text_in = send(text_embed, chip_mate)
    image_in = send(image_embed, chip_mate)

    image_low, text_low, image_sum, text_sum, loss = call(
        own_kernel, (low, low, wide, wide, lanes), [held, held], scalars,
        (image_embed, text_embed, image_in, text_in),
    )
    image_sum, loss = call(
        text_kernel, (wide, lanes), [held], scalars, (text_y, image_low, image_sum, loss)
    )
    image_grad, text_sum, loss = call(
        group_kernel, (low, wide, jax.ShapeDtypeStruct((rows, 1), jnp.float32)), [held, held], scalars,
        (text_z, image_z, image_embed, image_low, text_low, image_sum, text_sum, loss),
    )
    (text_grad,) = call(
        last_kernel, (low,), [held], scalars, (image_y, text_embed, text_low, text_sum)
    )
    return (image_grad, text_grad, loss.reshape(rows))


def solution(mesh):
    placed = (P(AXES, None), P(AXES, None), P(), P())
    return jax.shard_map(
        on_device,
        mesh=mesh,
        in_specs=placed,
        out_specs=(P(AXES, None), P(AXES, None), P(AXES)),
        check_vma=False,
    )
```

```python
import jax
import jax.numpy as jnp
from jax import lax
from jax.experimental import pallas as pl
from jax.experimental.pallas import tpu as pltpu
from jax.sharding import PartitionSpec as P

AXES = ("grp", "blk")
N_GRP = 16
N_BLK = 32
PLANES = 8
TILE = 512
VMEM = pl.BlockSpec(memory_space=pltpu.VMEM)
HBM = pl.BlockSpec(memory_space=pltpu.HBM)
PIECE = 128
UPPER_PLANES = (1, 0)
LOWER_PLANES = (2, 3)
VMEM_LIMIT = 20 * 1024 * 1024
SMEM = pl.BlockSpec(memory_space=pltpu.SMEM)


def pairs(target):
    found = []
    for group in range(N_GRP):
        for block in range(N_BLK):
            to = target(group, block)
            if to is not None:
                found.append((group * N_BLK + block, (to[0] % N_GRP) * N_BLK + to[1] % N_BLK))
    return found


def send(array, target):
    return lax.ppermute(array, AXES, pairs(target))


def chip_mate(group, block):
    return (group, block ^ 1)


def across(group, block):
    return (group, block + 1 if block % 2 else block - 1)


def upward(group, block):
    return None if group % PLANES == PLANES - 1 else (group + 1, block)


def downward(group, block):
    return None if group % PLANES == 0 else (group - 1, block)


def same_way(group, block):
    return (block + group // PLANES) % 2 == 1


def to_relay(crossed, straight):
    def target(group, block):
        half, plane = divmod(group, PLANES)
        if plane not in (0, PLANES - 1):
            return None
        moved = same_way(group, block)
        place = crossed if moved else straight
        relay = place if plane else PLANES - 1 - place
        return (half * PLANES + relay, block ^ 1 if moved else block)

    return target


def from_relay(crossed, straight):
    def target(group, block):
        half, plane = divmod(group, PLANES)
        if same_way(group, block):
            return None
        for end, place in ((0, plane), (PLANES - 1, PLANES - 1 - plane)):
            if place in (crossed, straight):
                return ((1 - half) * PLANES + end, block ^ 1 if place == crossed else block)
        return None

    return target


def unit_rows(values):
    widened = values.astype(jnp.float32)
    inverse = lax.rsqrt(jnp.sum(widened * widened, axis=1, keepdims=True) + 1e-06)
    return (widened * inverse, inverse)


def scale_of(scale_ref):
    return jnp.exp(jnp.full((1, 1), scale_ref[0], jnp.float32))


def weights_of(logits, scale):
    half = 0.5 * scale
    return half * jnp.tanh(0.5 * logits) + half


def logits_of(left, right, scale, bias):
    scores = lax.dot_general(left, right, (((1,), (1,)), ((), ())), preferred_element_type=jnp.float32)
    return scale * scores + bias


def softplus(logits):
    return jnp.log(1.0 + jnp.exp(logits))


def lane_groups(values):
    total = values[:, :128]
    for start in range(128, values.shape[1], 128):
        total = total + values[:, start : start + 128]
    return total


def tangent(raw, summed):
    units, inverse = unit_rows(raw)
    inner = jnp.sum(units * summed, axis=1, keepdims=True)
    return (inverse * (summed - units * inner)).astype(jnp.bfloat16)


def diagonal(start, shape):
    rows = lax.broadcasted_iota(jnp.int32, shape, 0) + start
    return rows == lax.broadcasted_iota(jnp.int32, shape, 1)


def dot(left, right):
    return jnp.dot(left, right, preferred_element_type=jnp.float32)


def unit_kernel(image_ref, text_ref, pair_ref):
    rows = image_ref.shape[0]
    for start in range(0, rows, PIECE):
        here = pl.ds(start, PIECE)
        pair_ref[here, :] = unit_rows(image_ref[here, :])[0].astype(jnp.bfloat16)
        pair_ref[pl.ds(rows + start, PIECE), :] = unit_rows(text_ref[here, :])[0].astype(jnp.bfloat16)


def pick_kernel(pair_ref, pair_in_ref, upper_ref, lower_ref, image_out_ref, text_out_ref):
    del pair_in_ref
    low_plane = lax.axis_index("grp") % PLANES < PLANES // 2
    rows = image_out_ref.shape[0]
    half = rows // 2
    image_low, text_low = pair_ref[:rows, :], pair_ref[rows:, :]
    upper_ref[...] = jnp.where(low_plane, image_low[:half, :], text_low[:half, :])
    lower_ref[...] = jnp.where(low_plane, image_low[half:, :], text_low[half:, :])
    image_out_ref[...] = image_low
    text_out_ref[...] = text_low


def onward_kernel(relay_ref, after_ref, onward_ref):
    del after_ref
    onward_ref[...] = relay_ref[...]


def own_kernel(scale_ref, bias_ref, pair_ref, pair_in_ref, image_sum_ref, text_sum_ref, loss_ref):
    rows = image_sum_ref.shape[0]
    image_low_ref, text_low_ref = pair_ref.at[:rows, :], pair_ref.at[rows:, :]
    image_in_low, text_in_low = pair_in_ref.at[:rows, :], pair_in_ref.at[rows:, :]
    scale = scale_of(scale_ref)
    bias = bias_ref[0]

    @pl.loop(0, rows // TILE)
    def _(step):
        start = pl.multiple_of(step * TILE, TILE)
        here = pl.ds(start, TILE)
        image_low = image_low_ref[here, :]
        text_low = text_low_ref[here, :]
        logits = logits_of(image_low, text_low_ref[...], scale, bias)
        paired = diagonal(start, logits.shape)
        loss = lane_groups(softplus(jnp.where(paired, -logits, logits)))
        weights = (weights_of(logits, scale) - jnp.where(paired, scale, 0.0)).astype(jnp.bfloat16)
        image_sum = dot(weights, text_low_ref[...])
        logits = logits_of(image_low, text_in_low[...], scale, bias)
        loss_ref[here, :] = loss + lane_groups(softplus(logits))
        weights = weights_of(logits, scale).astype(jnp.bfloat16)
        image_sum_ref[here, :] = image_sum + dot(weights, text_in_low[...])
        logits = logits_of(text_low, image_low_ref[...], scale, bias)
        paired = diagonal(start, logits.shape)
        weights = (weights_of(logits, scale) - jnp.where(paired, scale, 0.0)).astype(jnp.bfloat16)
        text_sum = dot(weights, image_low_ref[...])
        logits = logits_of(text_low, image_in_low[...], scale, bias)
        weights = weights_of(logits, scale).astype(jnp.bfloat16)
        text_sum_ref[here, :] = text_sum + dot(weights, image_in_low[...])


def text_side(scale, bias, text_low, image_low_ref, image_sum_in, loss_in, image_sum_ref, loss_ref):
    logits = logits_of(image_low_ref[...], text_low, scale, bias)
    loss_ref[...] = loss_in[...] + lane_groups(softplus(logits))
    weights = weights_of(logits, scale).astype(jnp.bfloat16)
    image_sum_ref[...] = image_sum_in[...] + dot(weights, text_low)


def image_side(scale, bias, image_low, text_low_ref, text_sum_in, text_sum_ref):
    logits = logits_of(text_low_ref[...], image_low, scale, bias)
    weights = weights_of(logits, scale).astype(jnp.bfloat16)
    text_sum_ref[...] = text_sum_in[...] + dot(weights, image_low)


def mean_loss(loss, columns):
    return jnp.sum(loss.T, axis=0, keepdims=True) * (1.0 / columns)


def group_kernel(
    scale_ref, bias_ref, text_z_ref, image_z_ref, pair_ref, image_sum_in, text_sum_in, loss_in,
    image_sum_ref, text_sum_ref, loss_ref,
):
    rows = image_sum_ref.shape[0]
    image_low_ref, text_low_ref = pair_ref.at[:rows, :], pair_ref.at[rows:, :]
    scale = scale_of(scale_ref)
    bias = bias_ref[0]
    plane = lax.axis_index("grp") % PLANES

    @pl.when(plane != 0)
    def _():
        text_side(scale, bias, text_z_ref[...], image_low_ref, image_sum_in, loss_in, image_sum_ref, loss_ref)

    @pl.when(plane == 0)
    def _():
        image_sum_ref[...] = image_sum_in[...]
        loss_ref[...] = loss_in[...]

    @pl.when(plane != PLANES - 1)
    def _():
        image_side(scale, bias, image_z_ref[...], text_low_ref, text_sum_in, text_sum_ref)

    @pl.when(plane == PLANES - 1)
    def _():
        text_sum_ref[...] = text_sum_in[...]


def row_kernel(
    scale_ref, bias_ref, pair_y_ref, image_ref, text_ref, pair_ref, image_sum_in, text_sum_in,
    loss_in, image_grad_ref, text_grad_ref, image_sum_ref, text_sum_ref, loss_ref, row_loss_ref,
    image_raw, text_raw, image_grad, text_grad, reads, sems,
):
    copies = [
        pltpu.make_async_copy(image_ref, image_raw, reads.at[0]),
        pltpu.make_async_copy(text_ref, text_raw, reads.at[1]),
    ]
    for copy in copies:
        copy.start()
    scale = scale_of(scale_ref)
    bias = bias_ref[0]
    rows = image_ref.shape[0]
    plane = lax.axis_index("grp") % PLANES
    image_low_ref, text_low_ref = pair_ref.at[:rows, :], pair_ref.at[rows:, :]
    image_y_low, text_y_low = pair_y_ref[:rows, :], pair_y_ref[rows:, :]
    text_side(scale, bias, text_y_low, image_low_ref, image_sum_in, loss_in, image_sum_ref, loss_ref)
    row_loss_ref[...] = mean_loss(loss_ref[...], 4 * rows)
    writes = []
    for copy in copies:
        copy.wait()
    for start in range(0, rows, PIECE):
        here = pl.ds(start, PIECE)
        image_grad[here, :] = tangent(image_raw[here, :], image_sum_ref[here, :])
        writes.append(pltpu.make_async_copy(image_grad.at[here, :], image_grad_ref.at[here, :], sems.at[len(writes)]))
        writes[-1].start()
    image_side(scale, bias, image_y_low, text_low_ref, text_sum_in, text_sum_ref)
    for start in range(0, rows, PIECE):
        here = pl.ds(start, PIECE)
        text_grad[here, :] = tangent(text_raw[here, :], text_sum_ref[here, :])
        writes.append(pltpu.make_async_copy(text_grad.at[here, :], text_grad_ref.at[here, :], sems.at[len(writes)]))
        writes[-1].start()
    for copy in writes:
        copy.wait()


def far_kernel(
    scale_ref, bias_ref, upper_ref, lower_ref, image_ref, text_ref, pair_ref, image_sum_ref,
    text_sum_ref, loss_ref, row_loss_in, image_grad_in, text_grad_in, image_grad_ref, text_grad_ref, row_loss_ref,
    far, raw, summed, grad, read, sems,
):
    del image_grad_in, text_grad_in
    scale = scale_of(scale_ref)
    bias = bias_ref[0]
    rows = image_ref.shape[0]
    half = rows // 2
    image_low_ref, text_low_ref = pair_ref.at[:rows, :], pair_ref.at[rows:, :]
    plane = lax.axis_index("grp") % PLANES
    row_loss_ref[...] = row_loss_in[...]

    def finish(grad_ref):
        writes = []
        for start in range(0, rows, PIECE):
            here = pl.ds(start, PIECE)
            grad[here, :] = tangent(raw[here, :], summed[here, :])
            writes.append(pltpu.make_async_copy(grad.at[here, :], grad_ref.at[here, :], sems.at[len(writes)]))
            writes[-1].start()
        for copy in writes:
            copy.wait()

    @pl.when(plane == 0)
    def _():
        copy = pltpu.make_async_copy(image_ref, raw, read)
        copy.start()
        far[:half, :] = upper_ref[...]
        far[half:, :] = lower_ref[...]
        text_side(scale, bias, far[...], image_low_ref, image_sum_ref, loss_ref, summed, loss_ref)
        row_loss_ref[...] = mean_loss(loss_ref[...], 4 * rows)
        copy.wait()
        finish(image_grad_ref)

    @pl.when(plane == PLANES - 1)
    def _():
        copy = pltpu.make_async_copy(text_ref, raw, read)
        copy.start()
        far[:half, :] = upper_ref[...]
        far[half:, :] = lower_ref[...]
        image_side(scale, bias, far[...], text_low_ref, text_sum_ref, summed)
        copy.wait()
        finish(text_grad_ref)


def call(kernel, outs, scratch, scalars, arrays, in_hbm=(), out_hbm=(), aliases={}):
    return pl.pallas_call(
        kernel,
        out_shape=outs,
        in_specs=[SMEM] * len(scalars) + [HBM if i in in_hbm else VMEM for i in range(len(arrays))],
        out_specs=tuple(HBM if i in out_hbm else VMEM for i in range(len(outs))),
        scratch_shapes=scratch,
        input_output_aliases={len(scalars) + i: o for i, o in aliases.items()},
        compiler_params=pltpu.CompilerParams(vmem_limit_bytes=VMEM_LIMIT),
        cost_estimate=pl.CostEstimate(flops=1000, bytes_accessed=1000, transcendentals=0),
    )(*scalars, *arrays)


def some(rows, width=1152):
    return jax.ShapeDtypeStruct((rows, width), jnp.bfloat16)


def on_device(image_embed, text_embed, log_scale, bias):
    rows, width = image_embed.shape
    low = jax.ShapeDtypeStruct((rows, width), jnp.bfloat16)
    pair = jax.ShapeDtypeStruct((2 * rows, width), jnp.bfloat16)
    half = jax.ShapeDtypeStruct((rows // 2, width), jnp.bfloat16)
    wide = jax.ShapeDtypeStruct((rows, width), jnp.float32)
    lanes = jax.ShapeDtypeStruct((rows, 128), jnp.float32)
    held = pltpu.VMEM((rows, width), jnp.bfloat16)
    scalars = (log_scale, bias)

    (pair_low,) = call(unit_kernel, (pair,), [], (), (image_embed, text_embed))
    pair_in = send(pair_low, chip_mate)
    pair_y = send(pair_low, across)
    upper, lower, image_out, text_out = call(
        pick_kernel, (half, half, low, low), [], (), (pair_low, pair_in), (1,)
    )
    upper_relay = send(upper, to_relay(*UPPER_PLANES))
    lower_relay = send(lower, to_relay(*LOWER_PLANES))
    text_z = send(text_out, upward)
    image_z = send(image_out, downward)

    image_sum, text_sum, loss = call(
        own_kernel, (wide, wide, lanes), [], scalars, (pair_low, pair_in)
    )
    upper_far, lower_far = (
        send(call(onward_kernel, (half,), [], (), (relay, loss), (1,))[0], from_relay(*planes))
        for relay, planes in ((upper_relay, UPPER_PLANES), (lower_relay, LOWER_PLANES))
    )
    image_sum, text_sum, loss = call(
        group_kernel, (wide, wide, lanes), [], scalars,
        (text_z, image_z, pair_low, image_sum, text_sum, loss), aliases={3: 0, 4: 1, 5: 2},
    )
    row = jax.ShapeDtypeStruct((1, rows), jnp.float32)
    pieces = rows // PIECE
    image_grad, text_grad, image_sum, text_sum, loss, row_loss = call(
        row_kernel, (low, low, wide, wide, lanes, row),
        [held, held, held, held, pltpu.SemaphoreType.DMA((2,)), pltpu.SemaphoreType.DMA((2 * pieces,))], scalars,
        (pair_y, image_embed, text_embed, pair_low, image_sum, text_sum, loss),
        (1, 2), (0, 1), {4: 2, 5: 3, 6: 4},
    )
    image_grad, text_grad, loss = call(
        far_kernel, (low, low, row),
        [held, held, pltpu.VMEM((rows, width), jnp.float32), held, pltpu.SemaphoreType.DMA,
         pltpu.SemaphoreType.DMA((pieces,))], scalars,
        (upper_far, lower_far, image_embed, text_embed, pair_low, image_sum, text_sum, loss, row_loss,
         image_grad, text_grad),
        (2, 3, 9, 10), (0, 1), {9: 0, 10: 1},
    )
    return (image_grad, text_grad, loss.reshape(rows))


def solution(mesh):
    placed = (P(AXES, None), P(AXES, None), P(), P())
    return jax.shard_map(
        on_device,
        mesh=mesh,
        in_specs=placed,
        out_specs=(P(AXES, None), P(AXES, None), P(AXES)),
        check_vma=False,
    )
```

```python
import jax
import jax.numpy as jnp
from jax import lax
from jax.experimental import pallas as pl
from jax.experimental.pallas import tpu as pltpu
from jax.sharding import PartitionSpec as P

AXES = ("grp", "blk")
N_GRP = 16
N_BLK = 32
PLANES = 8
TILE = 512
VMEM = pl.BlockSpec(memory_space=pltpu.VMEM)
HBM = pl.BlockSpec(memory_space=pltpu.HBM)
PIECE = 128
UPPER_PLANES = (1, 0)
LOWER_PLANES = (2, 3)
VMEM_LIMIT = 20 * 1024 * 1024
SMEM = pl.BlockSpec(memory_space=pltpu.SMEM)


def pairs(target):
    found = []
    for group in range(N_GRP):
        for block in range(N_BLK):
            to = target(group, block)
            if to is not None:
                found.append((group * N_BLK + block, (to[0] % N_GRP) * N_BLK + to[1] % N_BLK))
    return found


def send(array, target):
    return lax.ppermute(array, AXES, pairs(target))


def chip_mate(group, block):
    return (group, block ^ 1)


def across(group, block):
    return (group, block + 1 if block % 2 else block - 1)


def upward(group, block):
    return None if group % PLANES == PLANES - 1 else (group + 1, block)


def downward(group, block):
    return None if group % PLANES == 0 else (group - 1, block)


def same_way(group, block):
    return (block + group // PLANES) % 2 == 1


def to_relay(crossed, straight):
    def target(group, block):
        half, plane = divmod(group, PLANES)
        if plane not in (0, PLANES - 1):
            return None
        moved = same_way(group, block)
        place = crossed if moved else straight
        relay = place if plane else PLANES - 1 - place
        return (half * PLANES + relay, block ^ 1 if moved else block)

    return target


def from_relay(crossed, straight):
    def target(group, block):
        half, plane = divmod(group, PLANES)
        if same_way(group, block):
            return None
        for end, place in ((0, plane), (PLANES - 1, PLANES - 1 - plane)):
            if place in (crossed, straight):
                return ((1 - half) * PLANES + end, block ^ 1 if place == crossed else block)
        return None

    return target


def unit_rows(values):
    widened = values.astype(jnp.float32)
    inverse = lax.rsqrt(jnp.sum(widened * widened, axis=1, keepdims=True) + 1e-06)
    return (widened * inverse, inverse)


def scale_of(scale_ref):
    return jnp.exp(jnp.full((1, 1), scale_ref[0], jnp.float32))


def weights_of(logits, scale):
    half = 0.5 * scale
    return half * jnp.tanh(0.5 * logits) + half


def logits_of(left, right, scale, bias):
    scores = lax.dot_general(left, right, (((1,), (1,)), ((), ())), preferred_element_type=jnp.float32)
    return scale * scores + bias


def softplus(logits):
    return jnp.log(1.0 + jnp.exp(logits))


def lane_groups(values):
    total = values[:, :128]
    for start in range(128, values.shape[1], 128):
        total = total + values[:, start : start + 128]
    return total


def tangent(raw, summed):
    units, inverse = unit_rows(raw)
    inner = jnp.sum(units * summed, axis=1, keepdims=True)
    return (inverse * (summed - units * inner)).astype(jnp.bfloat16)


def diagonal(start, shape):
    rows = lax.broadcasted_iota(jnp.int32, shape, 0) + start
    return rows == lax.broadcasted_iota(jnp.int32, shape, 1)


def dot(left, right):
    return jnp.dot(left, right, preferred_element_type=jnp.float32)


def unit_kernel(image_ref, text_ref, pair_ref, upper_ref, lower_ref, raw, sems):
    rows = image_ref.shape[0]
    half = rows // 2
    reads = []
    for source, base in ((image_ref, 0), (text_ref, rows)):
        for start in range(0, rows, PIECE):
            reads.append(
                pltpu.make_async_copy(
                    source.at[pl.ds(start, PIECE), :], raw.at[pl.ds(base + start, PIECE), :], sems.at[len(reads)]
                )
            )
            reads[-1].start()
    for step, read in enumerate(reads):
        here = pl.ds(step * PIECE, PIECE)
        read.wait()
        pair_ref[here, :] = unit_rows(raw[here, :])[0].astype(jnp.bfloat16)
    low_plane = lax.axis_index("grp") % PLANES < PLANES // 2
    upper_ref[...] = jnp.where(low_plane, pair_ref[:half, :], pair_ref[rows : rows + half, :])
    lower_ref[...] = jnp.where(low_plane, pair_ref[half:rows, :], pair_ref[rows + half :, :])


def parts_kernel(pair_ref, after_ref, image_ref, text_ref):
    del after_ref
    rows = image_ref.shape[0]
    image_ref[...] = pair_ref[:rows, :]
    text_ref[...] = pair_ref[rows:, :]


def onward_kernel(relay_ref, after_ref, onward_ref):
    del after_ref
    onward_ref[...] = relay_ref[...]


def own_kernel(scale_ref, bias_ref, pair_ref, pair_in_ref, image_sum_ref, text_sum_ref, loss_ref):
    rows = image_sum_ref.shape[0]
    image_low_ref, text_low_ref = pair_ref.at[:rows, :], pair_ref.at[rows:, :]
    image_in_low, text_in_low = pair_in_ref.at[:rows, :], pair_in_ref.at[rows:, :]
    scale = scale_of(scale_ref)
    bias = bias_ref[0]

    @pl.loop(0, rows // TILE)
    def _(step):
        start = pl.multiple_of(step * TILE, TILE)
        here = pl.ds(start, TILE)
        image_low = image_low_ref[here, :]
        text_low = text_low_ref[here, :]
        logits = logits_of(image_low, text_low_ref[...], scale, bias)
        paired = diagonal(start, logits.shape)
        loss = lane_groups(softplus(jnp.where(paired, -logits, logits)))
        weights = (weights_of(logits, scale) - jnp.where(paired, scale, 0.0)).astype(jnp.bfloat16)
        image_sum = dot(weights, text_low_ref[...])
        logits = logits_of(image_low, text_in_low[...], scale, bias)
        loss_ref[here, :] = loss + lane_groups(softplus(logits))
        weights = weights_of(logits, scale).astype(jnp.bfloat16)
        image_sum_ref[here, :] = image_sum + dot(weights, text_in_low[...])
        logits = logits_of(text_low, image_low_ref[...], scale, bias)
        paired = diagonal(start, logits.shape)
        weights = (weights_of(logits, scale) - jnp.where(paired, scale, 0.0)).astype(jnp.bfloat16)
        text_sum = dot(weights, image_low_ref[...])
        logits = logits_of(text_low, image_in_low[...], scale, bias)
        weights = weights_of(logits, scale).astype(jnp.bfloat16)
        text_sum_ref[here, :] = text_sum + dot(weights, image_in_low[...])


def text_side(scale, bias, text_low, image_low_ref, image_sum_in, loss_in, image_sum_ref, loss_ref):
    logits = logits_of(image_low_ref[...], text_low, scale, bias)
    loss_ref[...] = loss_in[...] + lane_groups(softplus(logits))
    weights = weights_of(logits, scale).astype(jnp.bfloat16)
    image_sum_ref[...] = image_sum_in[...] + dot(weights, text_low)


def image_side(scale, bias, image_low, text_low_ref, text_sum_in, text_sum_ref):
    logits = logits_of(text_low_ref[...], image_low, scale, bias)
    weights = weights_of(logits, scale).astype(jnp.bfloat16)
    text_sum_ref[...] = text_sum_in[...] + dot(weights, image_low)


def mean_loss(loss, columns):
    return jnp.sum(loss.T, axis=0, keepdims=True) * (1.0 / columns)


def group_kernel(
    scale_ref, bias_ref, text_z_ref, image_z_ref, pair_ref, image_sum_in, text_sum_in, loss_in,
    image_sum_ref, text_sum_ref, loss_ref,
):
    rows = image_sum_ref.shape[0]
    image_low_ref, text_low_ref = pair_ref.at[:rows, :], pair_ref.at[rows:, :]
    scale = scale_of(scale_ref)
    bias = bias_ref[0]
    plane = lax.axis_index("grp") % PLANES

    @pl.when(plane != 0)
    def _():
        text_side(scale, bias, text_z_ref[...], image_low_ref, image_sum_in, loss_in, image_sum_ref, loss_ref)

    @pl.when(plane == 0)
    def _():
        image_sum_ref[...] = image_sum_in[...]
        loss_ref[...] = loss_in[...]

    @pl.when(plane != PLANES - 1)
    def _():
        image_side(scale, bias, image_z_ref[...], text_low_ref, text_sum_in, text_sum_ref)

    @pl.when(plane == PLANES - 1)
    def _():
        text_sum_ref[...] = text_sum_in[...]


def row_kernel(
    scale_ref, bias_ref, pair_y_ref, image_ref, text_ref, pair_ref, image_sum_in, text_sum_in,
    loss_in, image_grad_ref, text_grad_ref, image_sum_ref, text_sum_ref, loss_ref, row_loss_ref,
    image_raw, text_raw, image_grad, text_grad, reads, sems,
):
    copies = [
        pltpu.make_async_copy(image_ref, image_raw, reads.at[0]),
        pltpu.make_async_copy(text_ref, text_raw, reads.at[1]),
    ]
    for copy in copies:
        copy.start()
    scale = scale_of(scale_ref)
    bias = bias_ref[0]
    rows = image_ref.shape[0]
    plane = lax.axis_index("grp") % PLANES
    image_low_ref, text_low_ref = pair_ref.at[:rows, :], pair_ref.at[rows:, :]
    image_y_low, text_y_low = pair_y_ref[:rows, :], pair_y_ref[rows:, :]
    text_side(scale, bias, text_y_low, image_low_ref, image_sum_in, loss_in, image_sum_ref, loss_ref)
    row_loss_ref[...] = mean_loss(loss_ref[...], 4 * rows)
    writes = []
    for copy in copies:
        copy.wait()
    for start in range(0, rows, PIECE):
        here = pl.ds(start, PIECE)
        image_grad[here, :] = tangent(image_raw[here, :], image_sum_ref[here, :])
        writes.append(pltpu.make_async_copy(image_grad.at[here, :], image_grad_ref.at[here, :], sems.at[len(writes)]))
        writes[-1].start()
    image_side(scale, bias, image_y_low, text_low_ref, text_sum_in, text_sum_ref)
    for start in range(0, rows, PIECE):
        here = pl.ds(start, PIECE)
        text_grad[here, :] = tangent(text_raw[here, :], text_sum_ref[here, :])
        writes.append(pltpu.make_async_copy(text_grad.at[here, :], text_grad_ref.at[here, :], sems.at[len(writes)]))
        writes[-1].start()
    for copy in writes:
        copy.wait()


def upper_kernel(
    scale_ref, bias_ref, upper_ref, pair_ref, image_sum_in, text_sum_in, loss_in, image_sum_ref, text_sum_ref, loss_ref
):
    scale = scale_of(scale_ref)
    bias = bias_ref[0]
    rows = image_sum_ref.shape[0]
    plane = lax.axis_index("grp") % PLANES

    @pl.when(plane == 0)
    def _():
        text_side(
            scale, bias, upper_ref[...], pair_ref.at[:rows, :], image_sum_in, loss_in, image_sum_ref, loss_ref
        )

    @pl.when(plane == PLANES - 1)
    def _():
        image_side(scale, bias, upper_ref[...], pair_ref.at[rows:, :], text_sum_in, text_sum_ref)


def far_kernel(
    scale_ref, bias_ref, lower_ref, image_ref, text_ref, pair_ref, image_sum_ref,
    text_sum_ref, loss_ref, row_loss_in, image_grad_in, text_grad_in, image_grad_ref, text_grad_ref, row_loss_ref,
    raw, summed, grad, read, sems,
):
    del image_grad_in, text_grad_in
    scale = scale_of(scale_ref)
    bias = bias_ref[0]
    rows = image_ref.shape[0]
    image_low_ref, text_low_ref = pair_ref.at[:rows, :], pair_ref.at[rows:, :]
    plane = lax.axis_index("grp") % PLANES
    row_loss_ref[...] = row_loss_in[...]

    def finish(grad_ref):
        writes = []
        for start in range(0, rows, PIECE):
            here = pl.ds(start, PIECE)
            grad[here, :] = tangent(raw[here, :], summed[here, :])
            writes.append(pltpu.make_async_copy(grad.at[here, :], grad_ref.at[here, :], sems.at[len(writes)]))
            writes[-1].start()
        for copy in writes:
            copy.wait()

    @pl.when(plane == 0)
    def _():
        copy = pltpu.make_async_copy(image_ref, raw, read)
        copy.start()
        text_side(scale, bias, lower_ref[...], image_low_ref, image_sum_ref, loss_ref, summed, loss_ref)
        row_loss_ref[...] = mean_loss(loss_ref[...], 4 * rows)
        copy.wait()
        finish(image_grad_ref)

    @pl.when(plane == PLANES - 1)
    def _():
        copy = pltpu.make_async_copy(text_ref, raw, read)
        copy.start()
        image_side(scale, bias, lower_ref[...], text_low_ref, text_sum_ref, summed)
        copy.wait()
        finish(text_grad_ref)


def call(kernel, outs, scratch, scalars, arrays, in_hbm=(), out_hbm=(), aliases={}, vmem=VMEM_LIMIT, flops=1000):
    return pl.pallas_call(
        kernel,
        out_shape=outs,
        in_specs=[SMEM] * len(scalars) + [HBM if i in in_hbm else VMEM for i in range(len(arrays))],
        out_specs=tuple(HBM if i in out_hbm else VMEM for i in range(len(outs))),
        scratch_shapes=scratch,
        input_output_aliases={len(scalars) + i: o for i, o in aliases.items()},
        compiler_params=pltpu.CompilerParams(vmem_limit_bytes=vmem),
        cost_estimate=pl.CostEstimate(flops=flops, bytes_accessed=1000, transcendentals=0),
    )(*scalars, *arrays)


def some(rows, width=1152):
    return jax.ShapeDtypeStruct((rows, width), jnp.bfloat16)


def on_device(image_embed, text_embed, log_scale, bias):
    rows, width = image_embed.shape
    low = jax.ShapeDtypeStruct((rows, width), jnp.bfloat16)
    pair = jax.ShapeDtypeStruct((2 * rows, width), jnp.bfloat16)
    half = jax.ShapeDtypeStruct((rows // 2, width), jnp.bfloat16)
    wide = jax.ShapeDtypeStruct((rows, width), jnp.float32)
    lanes = jax.ShapeDtypeStruct((rows, 128), jnp.float32)
    held = pltpu.VMEM((rows, width), jnp.bfloat16)
    scalars = (log_scale, bias)

    held_pair = pltpu.VMEM((2 * rows, width), jnp.bfloat16)
    fixed = [pltpu.with_memory_space_constraint(array, pltpu.HBM) for array in (image_embed, text_embed)]
    pair_low, upper, lower = call(
        unit_kernel, (pair, half, half), [held_pair, pltpu.SemaphoreType.DMA((2 * rows // PIECE,))], (), fixed,
        (0, 1),
    )
    pair_in = send(pair_low, chip_mate)
    pair_y = send(pair_low, across)
    image_out, text_out = call(parts_kernel, (low, low), [], (), (pair_low, pair_in), (1,))
    upper_relay = send(upper, to_relay(*UPPER_PLANES))
    lower_relay = send(lower, to_relay(*LOWER_PLANES))
    text_z = send(text_out, upward)
    image_z = send(image_out, downward)

    image_sum, text_sum, loss = call(
        own_kernel, (wide, wide, lanes), [], scalars, (pair_low, pair_in)
    )
    upper_far, lower_far = (
        send(call(onward_kernel, (half,), [], (), (relay, loss), (1,), flops=5000000000)[0], from_relay(*planes))
        for relay, planes in ((upper_relay, UPPER_PLANES), (lower_relay, LOWER_PLANES))
    )
    image_sum, text_sum, loss = call(
        group_kernel, (wide, wide, lanes), [], scalars,
        (text_z, image_z, pair_low, image_sum, text_sum, loss), aliases={3: 0, 4: 1, 5: 2},
    )
    row = jax.ShapeDtypeStruct((1, rows), jnp.float32)
    pieces = rows // PIECE
    image_grad, text_grad, image_sum, text_sum, loss, row_loss = call(
        row_kernel, (low, low, wide, wide, lanes, row),
        [held, held, held, held, pltpu.SemaphoreType.DMA((2,)), pltpu.SemaphoreType.DMA((2 * pieces,))], scalars,
        (pair_y, image_embed, text_embed, pair_low, image_sum, text_sum, loss),
        (1, 2), (0, 1), {4: 2, 5: 3, 6: 4},
    )
    image_sum, text_sum, loss = call(
        upper_kernel, (wide, wide, lanes), [], scalars, (upper_far, pair_low, image_sum, text_sum, loss),
        aliases={2: 0, 3: 1, 4: 2},
    )
    image_grad, text_grad, loss = call(
        far_kernel, (low, low, row),
        [held, pltpu.VMEM((rows, width), jnp.float32), held, pltpu.SemaphoreType.DMA,
         pltpu.SemaphoreType.DMA((pieces,))], scalars,
        (lower_far, image_embed, text_embed, pair_low, image_sum, text_sum, loss, row_loss,
         image_grad, text_grad),
        (1, 2, 8, 9), (0, 1), {8: 0, 9: 1},
    )
    return (image_grad, text_grad, loss.reshape(rows))


def solution(mesh):
    placed = (P(AXES, None), P(AXES, None), P(), P())
    return jax.shard_map(
        on_device,
        mesh=mesh,
        in_specs=placed,
        out_specs=(P(AXES, None), P(AXES, None), P(AXES)),
        check_vma=False,
    )
```

```python
import jax
import jax.numpy as jnp
from jax import lax
from jax.experimental import pallas as pl
from jax.experimental.pallas import tpu as pltpu
from jax.sharding import PartitionSpec as P

AXES = ("grp", "blk")
N_GRP = 16
N_BLK = 32
PLANES = 8
TILE = 512
VMEM = pl.BlockSpec(memory_space=pltpu.VMEM)
HBM = pl.BlockSpec(memory_space=pltpu.HBM)
PIECE = 128
UPPER_PLANES = (1, 0)
LOWER_PLANES = (2, 3)
VMEM_LIMIT = 20 * 1024 * 1024
SMEM = pl.BlockSpec(memory_space=pltpu.SMEM)


def pairs(target):
    found = []
    for group in range(N_GRP):
        for block in range(N_BLK):
            to = target(group, block)
            if to is not None:
                found.append((group * N_BLK + block, (to[0] % N_GRP) * N_BLK + to[1] % N_BLK))
    return found


def send(array, target):
    return lax.ppermute(array, AXES, pairs(target))


def chip_mate(group, block):
    return (group, block ^ 1)


def across(group, block):
    return (group, block + 1 if block % 2 else block - 1)


def upward(group, block):
    return None if group % PLANES == PLANES - 1 else (group + 1, block)


def downward(group, block):
    return None if group % PLANES == 0 else (group - 1, block)


def same_way(group, block):
    return (block + group // PLANES) % 2 == 1


def to_relay(crossed, straight):
    def target(group, block):
        half, plane = divmod(group, PLANES)
        if plane not in (0, PLANES - 1):
            return None
        moved = same_way(group, block)
        place = crossed if moved else straight
        relay = place if plane else PLANES - 1 - place
        return (half * PLANES + relay, block ^ 1 if moved else block)

    return target


def from_relay(crossed, straight):
    def target(group, block):
        half, plane = divmod(group, PLANES)
        if same_way(group, block):
            return None
        for end, place in ((0, plane), (PLANES - 1, PLANES - 1 - plane)):
            if place in (crossed, straight):
                return ((1 - half) * PLANES + end, block ^ 1 if place == crossed else block)
        return None

    return target


def unit_rows(values):
    widened = values.astype(jnp.float32)
    inverse = lax.rsqrt(jnp.sum(widened * widened, axis=1, keepdims=True) + 1e-06)
    return (widened * inverse, inverse)


def scale_of(scale_ref):
    return jnp.exp(jnp.full((1, 1), scale_ref[0], jnp.float32))


def weights_of(logits, scale):
    half = 0.5 * scale
    return half * jnp.tanh(0.5 * logits) + half


def logits_of(left, right, scale, bias):
    scores = lax.dot_general(left, right, (((1,), (1,)), ((), ())), preferred_element_type=jnp.float32)
    return scale * scores + bias


def softplus(logits):
    return jnp.log(1.0 + jnp.exp(logits))


def lane_groups(values):
    total = values[:, :128]
    for start in range(128, values.shape[1], 128):
        total = total + values[:, start : start + 128]
    return total


def tangent(raw, summed):
    units, inverse = unit_rows(raw)
    inner = jnp.sum(units * summed, axis=1, keepdims=True)
    return (inverse * (summed - units * inner)).astype(jnp.bfloat16)


def diagonal(start, shape):
    rows = lax.broadcasted_iota(jnp.int32, shape, 0) + start
    return rows == lax.broadcasted_iota(jnp.int32, shape, 1)


def dot(left, right):
    return jnp.dot(left, right, preferred_element_type=jnp.float32)


def unit_kernel(image_ref, text_ref, pair_ref, upper_ref, lower_ref, raw, sems):
    rows = image_ref.shape[0]
    half = rows // 2
    reads = []
    for source, base in ((image_ref, 0), (text_ref, rows)):
        for start in range(0, rows, PIECE):
            reads.append(
                pltpu.make_async_copy(
                    source.at[pl.ds(start, PIECE), :], raw.at[pl.ds(base + start, PIECE), :], sems.at[len(reads)]
                )
            )
            reads[-1].start()
    for step, read in enumerate(reads):
        here = pl.ds(step * PIECE, PIECE)
        read.wait()
        pair_ref[here, :] = unit_rows(raw[here, :])[0].astype(jnp.bfloat16)
    low_plane = lax.axis_index("grp") % PLANES < PLANES // 2
    upper_ref[...] = jnp.where(low_plane, pair_ref[:half, :], pair_ref[rows : rows + half, :])
    lower_ref[...] = jnp.where(low_plane, pair_ref[half:rows, :], pair_ref[rows + half :, :])


def parts_kernel(pair_ref, after_ref, image_ref, text_ref):
    del after_ref
    rows = image_ref.shape[0]
    image_ref[...] = pair_ref[:rows, :]
    text_ref[...] = pair_ref[rows:, :]


def onward_kernel(relay_ref, after_ref, onward_ref):
    del after_ref
    onward_ref[...] = relay_ref[...]


def own_kernel(scale_ref, bias_ref, pair_ref, pair_in_ref, image_sum_ref, text_sum_ref, loss_ref):
    rows = image_sum_ref.shape[0]
    image_low_ref, text_low_ref = pair_ref.at[:rows, :], pair_ref.at[rows:, :]
    image_in_low, text_in_low = pair_in_ref.at[:rows, :], pair_in_ref.at[rows:, :]
    scale = scale_of(scale_ref)
    bias = bias_ref[0]

    @pl.loop(0, rows // TILE)
    def _(step):
        start = pl.multiple_of(step * TILE, TILE)
        here = pl.ds(start, TILE)
        image_low = image_low_ref[here, :]
        text_low = text_low_ref[here, :]
        logits = logits_of(image_low, text_low_ref[...], scale, bias)
        paired = diagonal(start, logits.shape)
        loss = lane_groups(softplus(jnp.where(paired, -logits, logits)))
        weights = (weights_of(logits, scale) - jnp.where(paired, scale, 0.0)).astype(jnp.bfloat16)
        image_sum = dot(weights, text_low_ref[...])
        logits = logits_of(image_low, text_in_low[...], scale, bias)
        loss_ref[here, :] = loss + lane_groups(softplus(logits))
        weights = weights_of(logits, scale).astype(jnp.bfloat16)
        image_sum_ref[here, :] = image_sum + dot(weights, text_in_low[...])
        logits = logits_of(text_low, image_low_ref[...], scale, bias)
        paired = diagonal(start, logits.shape)
        weights = (weights_of(logits, scale) - jnp.where(paired, scale, 0.0)).astype(jnp.bfloat16)
        text_sum = dot(weights, image_low_ref[...])
        logits = logits_of(text_low, image_in_low[...], scale, bias)
        weights = weights_of(logits, scale).astype(jnp.bfloat16)
        text_sum_ref[here, :] = text_sum + dot(weights, image_in_low[...])


def text_side(scale, bias, text_low, image_low_ref, image_sum_in, loss_in, image_sum_ref, loss_ref):
    logits = logits_of(image_low_ref[...], text_low, scale, bias)
    loss_ref[...] = loss_in[...] + lane_groups(softplus(logits))
    weights = weights_of(logits, scale).astype(jnp.bfloat16)
    image_sum_ref[...] = image_sum_in[...] + dot(weights, text_low)


def image_side(scale, bias, image_low, text_low_ref, text_sum_in, text_sum_ref):
    logits = logits_of(text_low_ref[...], image_low, scale, bias)
    weights = weights_of(logits, scale).astype(jnp.bfloat16)
    text_sum_ref[...] = text_sum_in[...] + dot(weights, image_low)


def mean_loss(loss, columns):
    return jnp.sum(loss.T, axis=0, keepdims=True) * (1.0 / columns)


def group_kernel(
    scale_ref, bias_ref, text_z_ref, image_z_ref, pair_ref, image_sum_in, text_sum_in, loss_in,
    image_sum_ref, text_sum_ref, loss_ref,
):
    rows = image_sum_ref.shape[0]
    image_low_ref, text_low_ref = pair_ref.at[:rows, :], pair_ref.at[rows:, :]
    scale = scale_of(scale_ref)
    bias = bias_ref[0]
    plane = lax.axis_index("grp") % PLANES

    @pl.when(plane != 0)
    def _():
        text_side(scale, bias, text_z_ref[...], image_low_ref, image_sum_in, loss_in, image_sum_ref, loss_ref)

    @pl.when(plane == 0)
    def _():
        image_sum_ref[...] = image_sum_in[...]
        loss_ref[...] = loss_in[...]

    @pl.when(plane != PLANES - 1)
    def _():
        image_side(scale, bias, image_z_ref[...], text_low_ref, text_sum_in, text_sum_ref)

    @pl.when(plane == PLANES - 1)
    def _():
        text_sum_ref[...] = text_sum_in[...]


def row_kernel(
    scale_ref, bias_ref, pair_y_ref, image_ref, text_ref, pair_ref, image_sum_in, text_sum_in,
    loss_in, image_grad_ref, text_grad_ref, image_sum_ref, text_sum_ref, loss_ref, row_loss_ref,
    image_raw, text_raw, image_grad, text_grad, reads, sems,
):
    copies = [
        pltpu.make_async_copy(image_ref, image_raw, reads.at[0]),
        pltpu.make_async_copy(text_ref, text_raw, reads.at[1]),
    ]
    for copy in copies:
        copy.start()
    scale = scale_of(scale_ref)
    bias = bias_ref[0]
    rows = image_ref.shape[0]
    plane = lax.axis_index("grp") % PLANES
    image_low_ref, text_low_ref = pair_ref.at[:rows, :], pair_ref.at[rows:, :]
    image_y_low, text_y_low = pair_y_ref[:rows, :], pair_y_ref[rows:, :]
    text_side(scale, bias, text_y_low, image_low_ref, image_sum_in, loss_in, image_sum_ref, loss_ref)
    row_loss_ref[...] = mean_loss(loss_ref[...], 4 * rows)
    writes = []
    for copy in copies:
        copy.wait()
    for start in range(0, rows, PIECE):
        here = pl.ds(start, PIECE)
        image_grad[here, :] = tangent(image_raw[here, :], image_sum_ref[here, :])
        writes.append(pltpu.make_async_copy(image_grad.at[here, :], image_grad_ref.at[here, :], sems.at[len(writes)]))
        writes[-1].start()
    image_side(scale, bias, image_y_low, text_low_ref, text_sum_in, text_sum_ref)
    for start in range(0, rows, PIECE):
        here = pl.ds(start, PIECE)
        text_grad[here, :] = tangent(text_raw[here, :], text_sum_ref[here, :])
        writes.append(pltpu.make_async_copy(text_grad.at[here, :], text_grad_ref.at[here, :], sems.at[len(writes)]))
        writes[-1].start()
    for copy in writes:
        copy.wait()


def upper_kernel(
    scale_ref, bias_ref, upper_ref, pair_ref, image_sum_in, text_sum_in, loss_in, image_sum_ref, text_sum_ref, loss_ref
):
    scale = scale_of(scale_ref)
    bias = bias_ref[0]
    rows = image_sum_ref.shape[0]
    plane = lax.axis_index("grp") % PLANES

    @pl.when(plane == 0)
    def _():
        text_side(
            scale, bias, upper_ref[...], pair_ref.at[:rows, :], image_sum_in, loss_in, image_sum_ref, loss_ref
        )

    @pl.when(plane == PLANES - 1)
    def _():
        image_side(scale, bias, upper_ref[...], pair_ref.at[rows:, :], text_sum_in, text_sum_ref)


def far_kernel(
    scale_ref, bias_ref, lower_ref, image_ref, text_ref, pair_ref, image_sum_ref,
    text_sum_ref, loss_ref, row_loss_in, image_grad_in, text_grad_in, image_grad_ref, text_grad_ref, row_loss_ref,
    raw, summed, grad, read, sems,
):
    del image_grad_in, text_grad_in
    scale = scale_of(scale_ref)
    bias = bias_ref[0]
    rows = image_ref.shape[0]
    image_low_ref, text_low_ref = pair_ref.at[:rows, :], pair_ref.at[rows:, :]
    plane = lax.axis_index("grp") % PLANES
    row_loss_ref[...] = row_loss_in[...]

    half = rows // 2

    def finish(side, raw_source, grad_ref):
        copy = pltpu.make_async_copy(raw_source, raw, read)
        copy.start()
        writes = []
        for base in range(0, rows, half):
            side(pl.ds(base, half))
            if base == 0:
                copy.wait()
            for start in range(base, base + half, PIECE):
                here = pl.ds(start, PIECE)
                grad[here, :] = tangent(raw[here, :], summed[here, :])
                writes.append(pltpu.make_async_copy(grad.at[here, :], grad_ref.at[here, :], sems.at[len(writes)]))
                writes[-1].start()
        row_loss_ref[...] = mean_loss(loss_ref[...], 4 * rows)
        for copy in writes:
            copy.wait()

    @pl.when(plane == 0)
    def _():
        def side(here):
            text_side(
                scale, bias, lower_ref[...], image_low_ref.at[here, :], image_sum_ref.at[here, :],
                loss_ref.at[here, :], summed.at[here, :], loss_ref.at[here, :],
            )

        finish(side, image_ref, image_grad_ref)

    @pl.when(plane == PLANES - 1)
    def _():
        def side(here):
            image_side(
                scale, bias, lower_ref[...], text_low_ref.at[here, :], text_sum_ref.at[here, :], summed.at[here, :]
            )

        finish(side, text_ref, text_grad_ref)


def call(kernel, outs, scratch, scalars, arrays, in_hbm=(), out_hbm=(), aliases={}, vmem=VMEM_LIMIT, flops=1000):
    return pl.pallas_call(
        kernel,
        out_shape=outs,
        in_specs=[SMEM] * len(scalars) + [HBM if i in in_hbm else VMEM for i in range(len(arrays))],
        out_specs=tuple(HBM if i in out_hbm else VMEM for i in range(len(outs))),
        scratch_shapes=scratch,
        input_output_aliases={len(scalars) + i: o for i, o in aliases.items()},
        compiler_params=pltpu.CompilerParams(vmem_limit_bytes=vmem),
        cost_estimate=pl.CostEstimate(flops=flops, bytes_accessed=1000, transcendentals=0),
    )(*scalars, *arrays)


def some(rows, width=1152):
    return jax.ShapeDtypeStruct((rows, width), jnp.bfloat16)


def on_device(image_embed, text_embed, log_scale, bias):
    rows, width = image_embed.shape
    low = jax.ShapeDtypeStruct((rows, width), jnp.bfloat16)
    pair = jax.ShapeDtypeStruct((2 * rows, width), jnp.bfloat16)
    half = jax.ShapeDtypeStruct((rows // 2, width), jnp.bfloat16)
    wide = jax.ShapeDtypeStruct((rows, width), jnp.float32)
    lanes = jax.ShapeDtypeStruct((rows, 128), jnp.float32)
    held = pltpu.VMEM((rows, width), jnp.bfloat16)
    scalars = (log_scale, bias)

    held_pair = pltpu.VMEM((2 * rows, width), jnp.bfloat16)
    fixed = [pltpu.with_memory_space_constraint(array, pltpu.HBM) for array in (image_embed, text_embed)]
    pair_low, upper, lower = call(
        unit_kernel, (pair, half, half), [held_pair, pltpu.SemaphoreType.DMA((2 * rows // PIECE,))], (), fixed,
        (0, 1),
    )
    pair_in = send(pair_low, chip_mate)
    pair_y = send(pair_low, across)
    image_out, text_out = call(parts_kernel, (low, low), [], (), (pair_low, pair_in), (1,))
    upper_relay = send(upper, to_relay(*UPPER_PLANES))
    lower_relay = send(lower, to_relay(*LOWER_PLANES))
    text_z = send(text_out, upward)
    image_z = send(image_out, downward)

    image_sum, text_sum, loss = call(
        own_kernel, (wide, wide, lanes), [], scalars, (pair_low, pair_in)
    )
    upper_far, lower_far = (
        send(call(onward_kernel, (half,), [], (), (relay, loss), (1,), flops=5000000000)[0], from_relay(*planes))
        for relay, planes in ((upper_relay, UPPER_PLANES), (lower_relay, LOWER_PLANES))
    )
    image_sum, text_sum, loss = call(
        group_kernel, (wide, wide, lanes), [], scalars,
        (text_z, image_z, pair_low, image_sum, text_sum, loss), aliases={3: 0, 4: 1, 5: 2},
    )
    row = jax.ShapeDtypeStruct((1, rows), jnp.float32)
    pieces = rows // PIECE
    image_grad, text_grad, image_sum, text_sum, loss, row_loss = call(
        row_kernel, (low, low, wide, wide, lanes, row),
        [held, held, held, held, pltpu.SemaphoreType.DMA((2,)), pltpu.SemaphoreType.DMA((2 * pieces,))], scalars,
        (pair_y, image_embed, text_embed, pair_low, image_sum, text_sum, loss),
        (1, 2), (0, 1), {4: 2, 5: 3, 6: 4},
    )
    image_sum, text_sum, loss = call(
        upper_kernel, (wide, wide, lanes), [], scalars, (upper_far, pair_low, image_sum, text_sum, loss),
        aliases={2: 0, 3: 1, 4: 2},
    )
    image_grad, text_grad, loss = call(
        far_kernel, (low, low, row),
        [held, pltpu.VMEM((rows, width), jnp.float32), held, pltpu.SemaphoreType.DMA,
         pltpu.SemaphoreType.DMA((pieces,))], scalars,
        (lower_far, image_embed, text_embed, pair_low, image_sum, text_sum, loss, row_loss,
         image_grad, text_grad),
        (1, 2, 8, 9), (0, 1), {8: 0, 9: 1},
    )
    return (image_grad, text_grad, loss.reshape(rows))


def solution(mesh):
    placed = (P(AXES, None), P(AXES, None), P(), P())
    return jax.shard_map(
        on_device,
        mesh=mesh,
        in_specs=placed,
        out_specs=(P(AXES, None), P(AXES, None), P(AXES)),
        check_vma=False,
    )
```
